128 devices in a mesh: seq: 2 (over core), fsdp: 64 (over z, y, x).
Axes of the slice: x: 4, y: 4, z: 4, core: 2. Of those that a mesh axis runs over, the one named last changes fastest.
Arguments:
- latent_q: bfloat16 [8192, 1536], P(('seq', 'fsdp')), may hold values from -16 to 16
- latent_kv: bfloat16 [8192, 512], P(('seq', 'fsdp')), may hold values from -16 to 16
- grad_q_heads: bfloat16 [8192, 12288], P('seq', 'fsdp')
- grad_kv_heads: bfloat16 [8192, 16384], P('seq', 'fsdp')
- row_peak: float32 [64, 8192], P('fsdp', 'seq'), may hold values from 1 to 400
- momentum_q: float32 [64, 1536, 192], P('fsdp', 'seq'), may hold values from -6 to 6
- momentum_kv: float32 [64, 512, 256], P('fsdp', 'seq'), may hold values from -6 to 6
- weight_q: float32 [64, 1536, 192], P('fsdp', 'seq'), may hold values from -3 to 3
- weight_kv: float32 [64, 512, 256], P('fsdp', 'seq'), may hold values from -3 to 3
Outputs:
- new_momentum_q: float32 [64, 1536, 192], P('fsdp', 'seq')
- new_momentum_kv: float32 [64, 512, 256], P('fsdp', 'seq')
- update_q: float32 [64, 1536, 192], P('fsdp', 'seq')
- update_kv: float32 [64, 512, 256], P('fsdp', 'seq')
- new_weight_q: float32 [64, 1536, 192], P('fsdp', 'seq')
- new_weight_kv: float32 [64, 512, 256], P('fsdp', 'seq')
The draws below stay inside these ranges and needn't reach their ends.
All inputs are finite; a program needn't handle non-finite values.
Results may differ from the reference program's by a relative error of at most 0.0003.
Values may be sent and summed in bfloat16 or wider, within the bound.
No kernel may reach another device: no remote copies, remote signals or barrier semaphores. Data moves between devices by JAX's collectives and lax.ppermute only.
A program may use at most 128 MiB of HBM per device.

```python
import math
import jax
import jax.numpy as jnp
from jax import lax

HEADS = 64
QR = 1536
KR = 512
QN = 128
KN = 128
NS_STEPS = 5
TOKENS = 8192
QD = 192
KD = 256


def scale_table(key, num_rows, num_cols, spread):
    key_cols, key_rows = jax.random.split(key)
    col_scale = jnp.exp(jax.random.uniform(key_cols, (1, num_cols), jnp.float32) * jnp.log(10.0)) / 4.0
    row_scale = jnp.exp(jax.random.uniform(key_rows, (num_rows, 1), jnp.float32) * jnp.log(spread)) / jnp.sqrt(spread)
    return col_scale * row_scale


def scaled_field(key, num_rows, num_cols, factor):
    key_base, key_rest = jax.random.split(key)
    base = jnp.clip(jax.random.normal(key_base, (num_rows, num_cols), jnp.float32), -6.0, 6.0)
    spread = 1.0
    return base * scale_table(key_rest, num_rows, num_cols, spread) * factor


def draw_latent_q(key, part):
    key = jax.random.fold_in(key, 11)
    return scaled_field(key, TOKENS, QR, 1.0).astype(jnp.bfloat16)


def draw_latent_kv(key, part):
    key = jax.random.fold_in(key, 12)
    return scaled_field(key, TOKENS, KR, 1.0).astype(jnp.bfloat16)


def draw_grad_q_heads(key, part):
    key = jax.random.fold_in(key, 13)
    return scaled_field(key, TOKENS, HEADS * QD, TOKENS ** (-0.5)).astype(jnp.bfloat16)


def draw_grad_kv_heads(key, part):
    key = jax.random.fold_in(key, 14)
    return scaled_field(key, TOKENS, HEADS * KD, TOKENS ** (-0.5)).astype(jnp.bfloat16)


def draw_row_peak(key, part):
    key = jax.random.fold_in(key, 17)
    key_head, key_token = jax.random.split(key)
    head_scale = jnp.exp(jax.random.uniform(key_head, (HEADS, 1), jnp.float32, jnp.log(20.0), jnp.log(400.0)))
    position = jnp.arange(TOKENS, dtype=jnp.float32)[None, :] / TOKENS
    ramp = (1.0 + 2.0 * position) / 3.0
    uniform_part = jax.random.uniform(key_token, (HEADS, TOKENS), jnp.float32)
    shaped = 0.3 + 0.7 * uniform_part ** 6
    return (head_scale * ramp * shaped).astype(jnp.float32)


def steps_of(rng, dims, shards, smallest, high):
    level = 1.0
    for axis_at, blocks in shards:
        draws = jax.random.uniform(jax.random.fold_in(jax.random.fold_in(rng, 6), axis_at), (blocks,), jnp.float32, smallest / len(shards), high / len(shards))
        level = level * jnp.repeat(jnp.exp(draws), dims[axis_at] // blocks).reshape((-1,) + (1,) * (len(dims) - 1 - axis_at))
    return level


def noise(key, dims, width, bound, cuts=(), kind=jnp.bfloat16):
    entries = width * jax.random.normal(key, dims, jnp.float32)
    if cuts:
        entries = entries * steps_of(key, dims, cuts, -0.22, 0.18)
    return jnp.clip(entries, -bound, bound).astype(kind)


def setup_inputs(seed: int = 0) -> dict:
    key_list = jax.random.split(jax.random.key(seed), 10)
    latent_q = draw_latent_q(jax.random.fold_in(key_list[9], 71), 0)
    latent_kv = draw_latent_kv(jax.random.fold_in(key_list[9], 71), 0)
    grad_q_heads = draw_grad_q_heads(jax.random.fold_in(key_list[9], 71), 0)
    grad_kv_heads = draw_grad_kv_heads(jax.random.fold_in(key_list[9], 71), 0)
    row_peak = draw_row_peak(jax.random.fold_in(key_list[9], 71), 0)
    momentum_q = noise(key_list[5], (HEADS, QR, QD), 1.0, 6.0, ((0, 64), (1, 2)), jnp.float32)
    momentum_kv = noise(key_list[6], (HEADS, KR, KD), 1.0, 6.0, ((0, 64), (1, 2)), jnp.float32)
    weight_q = noise(key_list[7], (HEADS, QR, QD), 0.2, 3.0, ((0, 64), (1, 2)), jnp.float32)
    weight_kv = noise(key_list[8], (HEADS, KR, KD), 0.2, 3.0, ((0, 64), (1, 2)), jnp.float32)
    return {"latent_q": latent_q, "latent_kv": latent_kv, "grad_q_heads": grad_q_heads, "grad_kv_heads": grad_kv_heads, "row_peak": row_peak, "momentum_q": momentum_q, "momentum_kv": momentum_kv, "weight_q": weight_q, "weight_kv": weight_kv}


coef_a = 3.4445
coef_b = -4.775
coef_c = 2.0315
momentum_rate = 0.95
learn_rate = 0.1
clip_target = 100.0
norm_eps = 1e-07

def batched(spec, left, right):
    return jnp.einsum(spec, left, right, precision=lax.Precision.HIGHEST)

def orthogonalize(matrix):
    norm = jnp.sqrt(lax.optimization_barrier(jnp.sum(matrix * matrix, axis=(1, 2), keepdims=True)))
    iterate = matrix / (norm + norm_eps)
    for sweep in range(NS_STEPS):
        gram = batched('nrc,nrd->ncd', iterate, iterate)
        poly = coef_b * gram + coef_c * batched('ncd,nde->nce', gram, gram)
        iterate = coef_a * iterate + batched('nrc,ncd->nrd', iterate, poly)
    return iterate

def head_grads(latent, grad_out, head_width):
    whole = lax.dot_general(latent, grad_out, (((0,), (0,)), ((), ())), preferred_element_type=jnp.float32)
    return whole.reshape(latent.shape[1], HEADS, head_width).transpose(1, 0, 2)

def reference(latent_q, latent_kv, grad_q_heads, grad_kv_heads, row_peak, momentum_q, momentum_kv, weight_q, weight_kv):
    grad_q = head_grads(latent_q, grad_q_heads, QD)
    grad_kv = head_grads(latent_kv, grad_kv_heads, KD)
    new_momentum_q = momentum_rate * momentum_q + grad_q
    new_momentum_kv = momentum_rate * momentum_kv + grad_kv
    update_q = 0.2 * math.sqrt(QR) * orthogonalize(new_momentum_q)
    update_kv = 0.2 * math.sqrt(KR) * orthogonalize(new_momentum_kv)
    peak = lax.optimization_barrier(jnp.max(row_peak, axis=1))
    factor = jnp.minimum(1.0, clip_target / peak)
    root = jnp.sqrt(factor)
    scale_q = jnp.where(jnp.arange(QD)[None, :] < QN, root[:, None], factor[:, None])
    scale_kv = jnp.where(jnp.arange(KD)[None, :] < KN, root[:, None], jnp.ones_like(root)[:, None])
    new_weight_q = (weight_q - learn_rate * update_q) * scale_q[:, None, :]
    new_weight_kv = (weight_kv - learn_rate * update_kv) * scale_kv[:, None, :]
    return (new_momentum_q, new_momentum_kv, update_q, update_kv, new_weight_q, new_weight_kv)
```

```python
import functools
import math

import jax
import jax.numpy as jnp
from jax import lax
from jax.experimental import pallas as pl
from jax.experimental.pallas import tpu as pltpu
from jax.sharding import PartitionSpec as P

QN = 128
KN = 128
NS_STEPS = 5

coef_a = 3.4445
coef_b = -4.775
coef_c = 2.0315
momentum_rate = 0.95
learn_rate = 0.1
clip_target = 100.0
norm_eps = 1e-07

F32 = jnp.float32
BF16 = jnp.bfloat16


def dot(left, right, left_dim=1, right_dim=0):
    return lax.dot_general(
        left, right, (((left_dim,), (right_dim,)), ((), ())), preferred_element_type=F32
    )


def halves(value):
    high = value.astype(BF16)
    return high, (value - high.astype(F32)).astype(BF16)


def product(left, right):
    (lh, ll), (rh, rl) = left, right
    return dot(lh, rh) + (dot(lh, rl) + dot(ll, rh))


def gram_of(parts):
    high, low = parts
    cross = dot(high, low, 1, 1)
    return dot(high, high, 1, 1) + (cross + cross.T)


def sweep(iterate):
    parts = halves(iterate)
    gram = gram_of(parts)
    gram_parts = halves(gram)
    poly = coef_b * gram + coef_c * product(gram_parts, gram_parts)
    return coef_a * iterate + product(halves(poly), parts)


def normalized(matrix):
    norm = jnp.sqrt(jnp.sum(matrix * matrix))
    return matrix / (norm + norm_eps)


def finish_kernel(
    core_ref,
    root_ref,
    factor_ref,
    own_q_ref,
    other_q_ref,
    mom_q_ref,
    weight_q_ref,
    own_kv_ref,
    other_kv_ref,
    mom_kv_ref,
    weight_kv_ref,
    out_mom_q_ref,
    out_mom_kv_ref,
    out_upd_q_ref,
    out_upd_kv_ref,
    out_weight_q_ref,
    out_weight_kv_ref,
    full_q_ref,
    full_kv_ref,
):
    core = core_ref[0]
    root = root_ref[0]
    factor = factor_ref[0]
    shard_q = out_mom_q_ref.shape[1]
    shard_kv = out_mom_kv_ref.shape[0]
    cols_q = pl.ds(pl.multiple_of(core * shard_q, 128), shard_q)
    cols_kv = pl.ds(pl.multiple_of(core * shard_kv, 128), shard_kv)
    mom_q = momentum_rate * mom_q_ref[...] + (own_q_ref[...] + other_q_ref[...])
    mom_kv = momentum_rate * mom_kv_ref[...] + (own_kv_ref[...] + other_kv_ref[...])
    full_q_ref[...] = mom_q
    full_kv_ref[...] = mom_kv
    out_mom_q_ref[...] = full_q_ref[:, cols_q]
    out_mom_kv_ref[...] = full_kv_ref[:, cols_kv].T
    x_q = normalized(mom_q)
    x_kv = normalized(mom_kv)
    for _ in range(NS_STEPS):
        x_q = sweep(x_q)
        x_kv = sweep(x_kv)
    full_q_ref[...] = x_q
    full_kv_ref[...] = x_kv
    upd_q = (0.2 * math.sqrt(x_q.shape[1])) * full_q_ref[:, cols_q]
    out_upd_q_ref[...] = upd_q
    rows = lax.broadcasted_iota(jnp.int32, upd_q.shape, 0)
    scale_q = jnp.where(rows < QN, root, factor)
    out_weight_q_ref[...] = (weight_q_ref[...] - learn_rate * upd_q) * scale_q
    upd_kv = ((0.2 * math.sqrt(x_kv.shape[1])) * full_kv_ref[:, cols_kv]).T
    out_upd_kv_ref[...] = upd_kv
    lanes = lax.broadcasted_iota(jnp.int32, upd_kv.shape, 1)
    scale_kv = jnp.where(lanes < KN, root, 1.0)
    out_weight_kv_ref[...] = (weight_kv_ref[...] - learn_rate * upd_kv) * scale_kv


def finish(core, root, factor, *arrays):
    own_q, _, _, weight_q, own_kv, _, _, weight_kv = arrays
    smem = pl.BlockSpec(memory_space=pltpu.SMEM)
    vmem = pl.BlockSpec(memory_space=pltpu.VMEM)
    shape_q = jax.ShapeDtypeStruct(weight_q.shape, F32)
    shape_kv = jax.ShapeDtypeStruct(weight_kv.shape, F32)
    return pl.pallas_call(
        finish_kernel,
        out_shape=(shape_q, shape_kv) * 3,
        in_specs=[smem] * 3 + [vmem] * 8,
        out_specs=(vmem,) * 6,
        scratch_shapes=[pltpu.VMEM(own_q.shape, F32), pltpu.VMEM(own_kv.shape, F32)],
        compiler_params=pltpu.CompilerParams(vmem_limit_bytes=48 * 1024 * 1024),
        cost_estimate=pl.CostEstimate(
            flops=20_000_000_000, bytes_accessed=12_000_000, transcendentals=0
        ),
    )(core, root, factor, *arrays)


def swap(value):
    return lax.ppermute(value, "seq", [(0, 1), (1, 0)])


def joined(core, own, axis):
    other = swap(own)
    return jnp.where(
        core == 0,
        jnp.concatenate([own, other], axis=axis),
        jnp.concatenate([other, own], axis=axis),
    )


def on_device(
    latent_q,
    latent_kv,
    grad_q_heads,
    grad_kv_heads,
    row_peak,
    momentum_q,
    momentum_kv,
    weight_q,
    weight_kv,
):
    core = lax.axis_index("seq")
    rank_q = latent_q.shape[1]
    latents = lax.all_gather(
        jnp.concatenate([latent_q, latent_kv], axis=1), "fsdp", axis=0, tiled=True
    )
    peak_own = jnp.max(row_peak, axis=1)
    peak = jnp.maximum(peak_own, swap(peak_own))
    factor = jnp.minimum(1.0, clip_target / peak)
    root = jnp.sqrt(factor)
    mom_q = joined(core, momentum_q[0].T, 1)
    mom_kv = joined(core, momentum_kv[0].T, 1)
    own_q = dot(grad_q_heads.T, latents[:, :rank_q])
    own_kv = dot(grad_kv_heads.T, latents[:, rank_q:])
    outs = finish(
        core.reshape(1),
        root,
        factor,
        own_q,
        swap(own_q),
        mom_q,
        weight_q[0].T,
        own_kv,
        swap(own_kv),
        mom_kv,
        weight_kv[0],
    )
    new_mom_q, new_mom_kv, upd_q, upd_kv, new_weight_q, new_weight_kv = outs
    return (
        new_mom_q.T[None],
        new_mom_kv[None],
        upd_q.T[None],
        upd_kv[None],
        new_weight_q.T[None],
        new_weight_kv[None],
    )


def solution(mesh):
    rows = P("fsdp", "seq", None)
    placed = (
        P(("seq", "fsdp"), None),
        P(("seq", "fsdp"), None),
        P("seq", "fsdp"),
        P("seq", "fsdp"),
        P("fsdp", "seq"),
        rows,
        rows,
        rows,
        rows,
    )
    return jax.shard_map(
        on_device, mesh=mesh, in_specs=placed, out_specs=(rows,) * 6, check_vma=False
    )
```

```python
import functools
import math

import jax
import jax.numpy as jnp
import numpy as np
from jax import lax
from jax.experimental import pallas as pl
from jax.experimental.pallas import tpu as pltpu
from jax.sharding import PartitionSpec as P

QN = 128
KN = 128
NS_STEPS = 5

coef_a = 3.4445
coef_b = -4.775
coef_c = 2.0315
momentum_rate = 0.95
learn_rate = 0.1
clip_target = 100.0
norm_eps = 1e-07

F32 = jnp.float32
BF16 = jnp.bfloat16

CHIPS = 64
RING = 4
PARTS = 3
STRIDES = {"z": 16, "y": 4, "x": 1}
AXES = (("xyz", "yzx", "zxy"), ("yzx", "zxy", "xyz"))
HOPS = ((1, 3), (3, 1))
SMEM = pl.BlockSpec(memory_space=pltpu.SMEM)
VMEM = pl.BlockSpec(memory_space=pltpu.VMEM)
MIB = 1024 * 1024


def dot(left, right, left_dim=1, right_dim=0):
    return lax.dot_general(
        left, right, (((left_dim,), (right_dim,)), ((), ())), preferred_element_type=F32
    )


def halves(value):
    high = value.astype(BF16)
    return high, (value - high.astype(F32)).astype(BF16)


def product(left, right):
    (lh, ll), (rh, rl) = left, right
    return dot(lh, rh) + (dot(lh, rl) + dot(ll, rh))


def gram_of(parts):
    high, low = parts
    cross = dot(high, low, 1, 1)
    return dot(high, high, 1, 1) + (cross + cross.T)


def sweep(iterate):
    parts = halves(iterate)
    gram = gram_of(parts)
    gram_parts = halves(gram)
    poly = coef_b * gram + coef_c * product(gram_parts, gram_parts)
    return coef_a * iterate + product(halves(poly), parts)


def normalized(matrix):
    norm = jnp.sqrt(jnp.sum(matrix * matrix, keepdims=True))
    return matrix / (norm + norm_eps)


class Layout:
    def __init__(self, width_q, width_kv, rank_q, rank_kv):
        unit_q, unit_kv = rank_q // PARTS, rank_kv // 4
        starts = (0, 2, 3, 4)
        self.width_q, self.width_kv = width_q, width_kv
        self.rank_q, self.rank_kv = rank_q, rank_kv
        self.q = [(p * unit_q, unit_q) for p in range(PARTS)]
        self.kv = [
            (starts[p] * unit_kv, (starts[p + 1] - starts[p]) * unit_kv) for p in range(PARTS)
        ]
        self.pack_width = unit_q

    def bands(self, part):
        wide = self.kv[part][1]
        count = self.pack_width // wide
        tall = self.width_kv // count
        return [(i * tall, tall, i * wide, wide) for i in range(count)]

    def pack_shape(self, part):
        return (self.width_q + self.bands(part)[0][1], self.pack_width)


def swap(value):
    return lax.ppermute(value, "seq", [(0, 1), (1, 0)])


def after(values, earlier):
    return lax.optimization_barrier((values, earlier))[0]


def exchange(value, part, phase, step):
    pairs = []
    for core in range(2):
        stride = STRIDES[AXES[core][part][phase]]
        for chip in range(CHIPS):
            at = chip // stride % RING
            other = chip + ((at ^ HOPS[core][step]) - at) * stride
            pairs.append((core * CHIPS + chip, core * CHIPS + other))
    return lax.ppermute(value, ("seq", "fsdp"), pairs)


def block_orders():
    table = np.zeros((2 * CHIPS, PARTS * CHIPS), np.int32)
    for core in range(2):
        first, second = HOPS[core]
        order = (0, first, second, first ^ second)
        for chip in range(CHIPS):
            for part in range(PARTS):
                for slot in range(CHIPS):
                    chosen = chip
                    for phase in range(3):
                        stride = STRIDES[AXES[core][part][phase]]
                        at = chip // stride % RING
                        turn = order[slot // RING**phase % RING]
                        chosen += ((at ^ turn) - at) * stride
                    table[core * CHIPS + chip, part * CHIPS + slot] = chosen
    return table


def arrange_kernel(order_ref, grad_q_ref, grad_kv_ref, *outs):
    rows = grad_kv_ref.shape[0] // CHIPS
    width_q = grad_q_ref.shape[0]
    pair = 2 * rows
    left = lax.broadcasted_iota(jnp.int32, (width_q, pair), 1) < rows

    def query_pair(first, second):
        turned = []
        for block, half in ((first, 0), (second, 1)):
            tile = grad_q_ref[:, pl.ds(pl.multiple_of(block // 2 * pair, pair), pair)]
            tile = tile.astype(F32)
            turned.append(jnp.where(block % 2 == half, tile, pltpu.roll(tile, rows, 1)))
        return jnp.where(left, turned[0], turned[1]).astype(BF16)

    for part in range(PARTS):
        for slot in range(RING):
            out = outs[part + PARTS * (slot % 2)]

            @pl.loop(0, RING)
            def _(chunk):
                base = part * CHIPS + slot * 16 + chunk * RING
                start = (slot // 2) * 16 * rows + chunk * (RING * rows)
                at = [order_ref[base + k] for k in range(RING)]
                for k in range(0, RING, 2):
                    lanes = pl.ds(pl.multiple_of(start + k * rows, pair), pair)
                    out[:width_q, lanes] = query_pair(at[k], at[k + 1])
                spans = [pl.ds(pl.multiple_of(block * rows, rows), rows) for block in at]
                whole = jnp.concatenate([grad_kv_ref[span, :] for span in spans], axis=0)
                lanes = pl.ds(pl.multiple_of(start, RING * rows), RING * rows)
                out[width_q:, lanes] = whole.T


def arrange(order, grad_q, grad_kv):
    shape = (grad_q.shape[0] + grad_kv.shape[1], grad_kv.shape[0] // 2)
    outs = pl.pallas_call(
        arrange_kernel,
        out_shape=(jax.ShapeDtypeStruct(shape, BF16),) * (2 * PARTS),
        in_specs=[SMEM, VMEM, VMEM],
        out_specs=(VMEM,) * (2 * PARTS),
        compiler_params=pltpu.CompilerParams(vmem_limit_bytes=24 * MIB),
        cost_estimate=pl.CostEstimate(
            flops=0, bytes_accessed=20_000_000, transcendentals=0
        ),
    )(order, grad_q, grad_kv)
    return outs[:PARTS], outs[PARTS:]


def multiply_kernel(layout, half, count_in, *refs):
    pieces, grads = refs[:PARTS], refs[PARTS : 2 * PARTS]
    sums, outs = refs[2 * PARTS : 2 * PARTS + count_in], refs[-PARTS:]
    span = pieces[0].shape[0]
    lanes = pl.ds(half * span, span)
    tall_q = layout.width_q
    for part in range(PARTS):
        wide_q = layout.q[part][1]
        term_q = dot(grads[part][:tall_q, lanes], pieces[part][:, :wide_q])
        term_kv = dot(grads[part][tall_q:, lanes], pieces[part][:, wide_q:])
        spots = [((0, tall_q), (0, wide_q), term_q)]
        for top, tall, at, wide in layout.bands(part):
            spots.append(((tall_q, tall), (at, wide), term_kv[top : top + tall, :]))
        for rows, cols, term in spots:
            where = (pl.ds(*rows), pl.ds(*cols))
            outs[part][where] = term + sums[part][where] if count_in else term


def multiply(layout, half, pieces, grads, sums=()):
    operands = [*pieces, *grads, *sums]
    return pl.pallas_call(
        functools.partial(multiply_kernel, layout, half, len(sums)),
        out_shape=tuple(
            jax.ShapeDtypeStruct(layout.pack_shape(p), F32) for p in range(PARTS)
        ),
        in_specs=[VMEM] * len(operands),
        out_specs=(VMEM,) * PARTS,
        compiler_params=pltpu.CompilerParams(vmem_limit_bytes=32 * MIB),
        cost_estimate=pl.CostEstimate(
            flops=2_000_000_000, bytes_accessed=8_000_000, transcendentals=0
        ),
    )(*operands)


def finish_kernel(layout, core_ref, *refs):
    packs = [refs[i * PARTS : (i + 1) * PARTS] for i in range(4)]
    (
        peak_ref,
        peak_other_ref,
        mom_q_ref,
        mom_q_other_ref,
        mom_kv_ref,
        mom_kv_other_ref,
        weight_q_ref,
        weight_kv_ref,
        out_mom_q_ref,
        out_mom_kv_ref,
        out_upd_q_ref,
        out_upd_kv_ref,
        out_weight_q_ref,
        out_weight_kv_ref,
        full_q_ref,
        full_kv_ref,
    ) = refs[4 * PARTS :]
    core = core_ref[0]
    peak = jnp.maximum(
        jnp.max(peak_ref[...], keepdims=True), jnp.max(peak_other_ref[...], keepdims=True)
    )
    factor = jnp.minimum(1.0, clip_target / peak)
    root = jnp.sqrt(factor)

    def lanes(at, ref):
        return pl.ds(pl.multiple_of(at * ref.shape[1] // 2, 128), ref.shape[1] // 2)

    own_q, other_q = lanes(core, full_q_ref), lanes(1 - core, full_q_ref)
    own_kv, other_kv = lanes(core, full_kv_ref), lanes(1 - core, full_kv_ref)
    full_q_ref[:, own_q] = momentum_rate * mom_q_ref[...]
    full_q_ref[:, other_q] = momentum_rate * mom_q_other_ref[...]
    full_kv_ref[:, own_kv] = momentum_rate * mom_kv_ref[...].T
    full_kv_ref[:, other_kv] = momentum_rate * mom_kv_other_ref[...].T
    tall_q = layout.width_q
    for part in range(PARTS):
        own, own_swapped, got, got_swapped = [pack[part] for pack in packs]

        def total(rows, cols):
            where = (pl.ds(*rows), pl.ds(*cols))
            return (own[where] + own_swapped[where]) + (got[where] + got_swapped[where])

        at_q, wide_q = layout.q[part]
        full_q_ref[:, pl.ds(at_q, wide_q)] += total((0, tall_q), (0, wide_q))
        at_kv, wide_kv = layout.kv[part]
        for top, tall, at, wide in layout.bands(part):
            full_kv_ref[pl.ds(top, tall), pl.ds(at_kv, wide_kv)] += total(
                (tall_q, tall), (at, wide)
            )
    out_mom_q_ref[...] = full_q_ref[:, own_q]
    out_mom_kv_ref[...] = full_kv_ref[:, own_kv].T
    x_q = normalized(full_q_ref[...])
    x_kv = normalized(full_kv_ref[...])
    for _ in range(NS_STEPS):
        x_q = sweep(x_q)
        x_kv = sweep(x_kv)
    full_q_ref[...] = x_q
    full_kv_ref[...] = x_kv
    upd_q = (0.2 * math.sqrt(layout.rank_q)) * full_q_ref[:, own_q]
    out_upd_q_ref[...] = upd_q
    rows = lax.broadcasted_iota(jnp.int32, upd_q.shape, 0)
    scale_q = jnp.where(rows < QN, root, factor)
    out_weight_q_ref[...] = (weight_q_ref[...] - learn_rate * upd_q) * scale_q
    upd_kv = ((0.2 * math.sqrt(layout.rank_kv)) * full_kv_ref[:, own_kv]).T
    out_upd_kv_ref[...] = upd_kv
    columns = lax.broadcasted_iota(jnp.int32, upd_kv.shape, 1)
    scale_kv = jnp.where(columns < KN, root, 1.0)
    out_weight_kv_ref[...] = (weight_kv_ref[...] - learn_rate * upd_kv) * scale_kv


def finish(layout, core, packs, *arrays):
    weight_q, weight_kv = arrays[-2:]
    shape_q = jax.ShapeDtypeStruct(weight_q.shape, F32)
    shape_kv = jax.ShapeDtypeStruct(weight_kv.shape, F32)
    operands = [piece for pack in packs for piece in pack] + list(arrays)
    return pl.pallas_call(
        functools.partial(finish_kernel, layout),
        out_shape=(shape_q, shape_kv) * 3,
        in_specs=[SMEM] + [VMEM] * len(operands),
        out_specs=(VMEM,) * 6,
        scratch_shapes=[
            pltpu.VMEM((layout.width_q, layout.rank_q), F32),
            pltpu.VMEM((layout.width_kv, layout.rank_kv), F32),
        ],
        compiler_params=pltpu.CompilerParams(vmem_limit_bytes=40 * MIB),
        cost_estimate=pl.CostEstimate(
            flops=20_000_000_000, bytes_accessed=12_000_000, transcendentals=0
        ),
    )(core, *operands)


def on_device(
    latent_q,
    latent_kv,
    grad_q_heads,
    grad_kv_heads,
    row_peak,
    momentum_q,
    momentum_kv,
    weight_q,
    weight_kv,
):
    core = lax.axis_index("seq")
    device = core * CHIPS + lax.axis_index("fsdp")
    layout = Layout(
        momentum_q.shape[2], momentum_kv.shape[2], latent_q.shape[1], latent_kv.shape[1]
    )
    held = [
        jnp.concatenate(
            [latent_q[:, aq : aq + wq], latent_kv[:, ak : ak + wk]], axis=1
        )
        for (aq, wq), (ak, wk) in zip(layout.q, layout.kv)
    ]
    order = lax.dynamic_index_in_dim(jnp.asarray(block_orders()), device, keepdims=False)
    keep, send = arrange(order, grad_q_heads.T, grad_kv_heads)
    for phase in range(2):
        for step in range(2):
            if phase + step == 1:
                held = after(held, send[0])
            got = [exchange(held[p], p, phase, step) for p in range(PARTS)]
            got = lax.optimization_barrier(got)
            held = [jnp.concatenate([held[p], got[p]], axis=0) for p in range(PARTS)]
    partner = [exchange(send[p], p, 2, 0) for p in range(PARTS)]
    third = [exchange(held[p], p, 2, 1) for p in range(PARTS)]
    lent = multiply(layout, 0, held, partner)
    own = multiply(layout, 0, held, keep)
    lent = multiply(layout, 1, third, partner, lent)
    got = [exchange(lent[p], p, 2, 0) for p in range(PARTS)]
    own = multiply(layout, 1, third, keep, own)
    mom_q, mom_kv = momentum_q[0].T, momentum_kv[0]
    row_peak, mom_q, mom_kv = after((row_peak, mom_q, mom_kv), held[0])
    packs = (own, [swap(o) for o in own], got, [swap(g) for g in got])
    outs = finish(
        layout,
        core.reshape(1),
        packs,
        row_peak,
        swap(row_peak),
        mom_q,
        swap(mom_q),
        mom_kv,
        swap(mom_kv),
        weight_q[0].T,
        weight_kv[0],
    )
    new_mom_q, new_mom_kv, upd_q, upd_kv, new_weight_q, new_weight_kv = outs
    return (
        new_mom_q.T[None],
        new_mom_kv[None],
        upd_q.T[None],
        upd_kv[None],
        new_weight_q.T[None],
        new_weight_kv[None],
    )


def solution(mesh):
    rows = P("fsdp", "seq", None)
    placed = (
        P(("seq", "fsdp"), None),
        P(("seq", "fsdp"), None),
        P("seq", "fsdp"),
        P("seq", "fsdp"),
        P("fsdp", "seq"),
        rows,
        rows,
        rows,
        rows,
    )
    return jax.shard_map(
        on_device, mesh=mesh, in_specs=placed, out_specs=(rows,) * 6, check_vma=False
    )
```

```python
import functools
import math

import jax
import jax.numpy as jnp
import numpy as np
from jax import lax
from jax.experimental import pallas as pl
from jax.experimental.pallas import tpu as pltpu
from jax.sharding import PartitionSpec as P

QN = 128
KN = 128
NS_STEPS = 5

coef_a = 3.4445
coef_b = -4.775
coef_c = 2.0315
momentum_rate = 0.95
learn_rate = 0.1
clip_target = 100.0
norm_eps = 1e-07

F32 = jnp.float32
BF16 = jnp.bfloat16

CHIPS = 64
RING = 4
PARTS = 3
LENT = 2
STRIDES = {"z": 16, "y": 4, "x": 1}
AXES = (("xyz", "yzx", "zxy"), ("yzx", "zxy", "xyz"))
HOPS = ((1, 3), (3, 1))
SMEM = pl.BlockSpec(memory_space=pltpu.SMEM)
VMEM = pl.BlockSpec(memory_space=pltpu.VMEM)
MIB = 1024 * 1024


def dot(left, right, left_dim=1, right_dim=0):
    return lax.dot_general(
        left, right, (((left_dim,), (right_dim,)), ((), ())), preferred_element_type=F32
    )


def halves(value):
    high = value.astype(BF16)
    return high, (value - high.astype(F32)).astype(BF16)


def product(left, right):
    (lh, ll), (rh, rl) = left, right
    return dot(lh, rh) + (dot(lh, rl) + dot(ll, rh))


def gram_of(parts):
    high, low = parts
    cross = dot(high, low, 1, 1)
    return dot(high, high, 1, 1) + (cross + cross.T)


def sweep(iterate):
    parts = halves(iterate)
    gram = gram_of(parts)
    gram_parts = halves(gram)
    poly = coef_b * gram + coef_c * product(gram_parts, gram_parts)
    return coef_a * iterate + product(halves(poly), parts)


def normalized(matrix):
    norm = jnp.sqrt(jnp.sum(matrix * matrix, keepdims=True))
    return matrix / (norm + norm_eps)


def swap(value):
    return lax.ppermute(value, "seq", [(0, 1), (1, 0)])


def after(values, earlier):
    return lax.optimization_barrier((values, earlier))[0]


def exchange(value, part, phase, step):
    pairs = []
    for core in range(2):
        stride = STRIDES[AXES[core][part][phase]]
        for chip in range(CHIPS):
            at = chip // stride % RING
            other = chip + ((at ^ HOPS[core][step]) - at) * stride
            pairs.append((core * CHIPS + chip, core * CHIPS + other))
    return lax.ppermute(value, ("seq", "fsdp"), pairs)


def block_orders():
    table = np.zeros((2 * CHIPS, PARTS * CHIPS), np.int32)
    for core in range(2):
        first, second = HOPS[core]
        order = (0, first, second, first ^ second)
        for chip in range(CHIPS):
            for part in range(PARTS):
                for slot in range(CHIPS):
                    chosen = chip
                    for phase in range(3):
                        stride = STRIDES[AXES[core][part][phase]]
                        at = chip // stride % RING
                        turn = order[slot // RING**phase % RING]
                        chosen += ((at ^ turn) - at) * stride
                    table[core * CHIPS + chip, part * CHIPS + slot] = chosen
    return table


def arrange_kernel(first, order_ref, grad_ref, *outs):
    width, tokens = grad_ref.shape
    rows = tokens // CHIPS
    pair = 2 * rows
    left = lax.broadcasted_iota(jnp.int32, (width, pair), 1) < rows

    def joined(one, two):
        turned = []
        for block, half in ((one, 0), (two, 1)):
            tile = grad_ref[:, pl.ds(pl.multiple_of(block // 2 * pair, pair), pair)]
            tile = tile.astype(F32)
            turned.append(jnp.where(block % 2 == half, tile, pltpu.roll(tile, rows, 1)))
        return jnp.where(left, turned[0], turned[1]).astype(BF16)

    for part in range(LENT):
        for slot in (first, first + 2):

            @pl.loop(0, 8)
            def _(at):
                base = part * CHIPS + slot * 16 + at * 2
                lanes = pl.ds(pl.multiple_of((slot // 2 * 8 + at) * pair, pair), pair)
                outs[part][:, lanes] = joined(order_ref[base], order_ref[base + 1])


def arrange(first, order, grad):
    return pl.pallas_call(
        functools.partial(arrange_kernel, first),
        out_shape=(jax.ShapeDtypeStruct((grad.shape[0], grad.shape[1] // 2), BF16),) * LENT,
        in_specs=[SMEM, VMEM],
        out_specs=(VMEM,) * LENT,
        compiler_params=pltpu.CompilerParams(vmem_limit_bytes=12 * MIB),
        cost_estimate=pl.CostEstimate(
            flops=0, bytes_accessed=10_000_000, transcendentals=0
        ),
    )(order, grad)


def line_up_kernel(order_ref, grad_ref, out_ref):
    rows = grad_ref.shape[0] // CHIPS

    @pl.loop(0, CHIPS // RING)
    def _(chunk):
        base = (PARTS - 1) * CHIPS + chunk * RING
        at = [order_ref[base + k] for k in range(RING)]
        spans = [pl.ds(pl.multiple_of(block * rows, rows), rows) for block in at]
        whole = jnp.concatenate([grad_ref[span, :] for span in spans], axis=0)
        lanes = pl.ds(pl.multiple_of(chunk * (RING * rows), RING * rows), RING * rows)
        out_ref[:, lanes] = whole.T


def line_up(order, grad):
    return pl.pallas_call(
        line_up_kernel,
        out_shape=jax.ShapeDtypeStruct(grad.shape[::-1], BF16),
        in_specs=[SMEM, VMEM],
        out_specs=VMEM,
        compiler_params=pltpu.CompilerParams(vmem_limit_bytes=12 * MIB),
        cost_estimate=pl.CostEstimate(
            flops=0, bytes_accessed=10_000_000, transcendentals=0
        ),
    )(order, grad)


def multiply_kernel(slot, count, *refs):
    pieces, grads = refs[:count], refs[count : 2 * count]
    sums, outs = refs[2 * count : -count], refs[-count:]
    for i in range(count):
        span = pieces[i].shape[0]
        term = dot(grads[i][:, slot * span : (slot + 1) * span], pieces[i][...])
        outs[i][...] = term + sums[i][...] if sums else term


def multiply(slot, pieces, grads, sums=()):
    operands = [*pieces, *grads, *sums]
    count = len(pieces)
    return pl.pallas_call(
        functools.partial(multiply_kernel, slot, count),
        out_shape=tuple(
            jax.ShapeDtypeStruct((grad.shape[0], piece.shape[1]), F32)
            for grad, piece in zip(grads, pieces)
        ),
        in_specs=[VMEM] * len(operands),
        out_specs=(VMEM,) * count,
        compiler_params=pltpu.CompilerParams(vmem_limit_bytes=16 * MIB),
        cost_estimate=pl.CostEstimate(
            flops=2_000_000_000, bytes_accessed=8_000_000, transcendentals=0
        ),
    )(*operands)


def clip_factor(peak_ref, peak_other_ref):
    peak = jnp.maximum(
        jnp.max(peak_ref[...], keepdims=True), jnp.max(peak_other_ref[...], keepdims=True)
    )
    return jnp.minimum(1.0, clip_target / peak)


def shares(core_ref, full_ref):
    core, wide = core_ref[0], full_ref.shape[1] // 2
    return tuple(pl.ds(pl.multiple_of(at * wide, 128), wide) for at in (core, 1 - core))


def orthogonalized(full_ref):
    iterate = normalized(full_ref[...])
    for _ in range(NS_STEPS):
        iterate = sweep(iterate)
    full_ref[...] = iterate


def finish_q_kernel(core_ref, *refs):
    packs = [refs[i * LENT : (i + 1) * LENT] for i in range(4)]
    peak_ref, peak_other_ref, mom_ref, mom_other_ref, weight_ref = refs[4 * LENT : -4]
    out_mom_ref, out_upd_ref, out_weight_ref, full_ref = refs[-4:]
    own, other = shares(core_ref, full_ref)
    full_ref[:, own] = momentum_rate * mom_ref[...]
    full_ref[:, other] = momentum_rate * mom_other_ref[...]
    at = 0
    for one, one_swapped, two, two_swapped in zip(*packs):
        wide = one.shape[1]
        full_ref[:, at : at + wide] += (one[...] + one_swapped[...]) + (
            two[...] + two_swapped[...]
        )
        at += wide
    out_mom_ref[...] = full_ref[:, own]
    orthogonalized(full_ref)
    update = (0.2 * math.sqrt(full_ref.shape[1])) * full_ref[:, own]
    out_upd_ref[...] = update
    factor = clip_factor(peak_ref, peak_other_ref)
    rows = lax.broadcasted_iota(jnp.int32, update.shape, 0)
    scale = jnp.where(rows < QN, jnp.sqrt(factor), factor)
    out_weight_ref[...] = (weight_ref[...] - learn_rate * update) * scale


def finish_kv_kernel(core_ref, *refs):
    one, one_swapped, peak_ref, peak_other_ref, mom_ref, mom_other_ref, weight_ref = refs[:7]
    out_mom_ref, out_upd_ref, out_weight_ref, full_ref = refs[7:]
    own, other = shares(core_ref, full_ref)
    full_ref[:, own] = momentum_rate * mom_ref[...].T
    full_ref[:, other] = momentum_rate * mom_other_ref[...].T
    full_ref[...] += one[...] + one_swapped[...]
    out_mom_ref[...] = full_ref[:, own].T
    orthogonalized(full_ref)
    update = ((0.2 * math.sqrt(full_ref.shape[1])) * full_ref[:, own]).T
    out_upd_ref[...] = update
    root = jnp.sqrt(clip_factor(peak_ref, peak_other_ref))
    columns = lax.broadcasted_iota(jnp.int32, update.shape, 1)
    scale = jnp.where(columns < KN, root, 1.0)
    out_weight_ref[...] = (weight_ref[...] - learn_rate * update) * scale


def finish(kernel, full_shape, core, *arrays):
    shape = jax.ShapeDtypeStruct(arrays[-1].shape, F32)
    return pl.pallas_call(
        kernel,
        out_shape=(shape,) * 3,
        in_specs=[SMEM] + [VMEM] * len(arrays),
        out_specs=(VMEM,) * 3,
        scratch_shapes=[pltpu.VMEM(full_shape, F32)],
        compiler_params=pltpu.CompilerParams(vmem_limit_bytes=20 * MIB),
        cost_estimate=pl.CostEstimate(
            flops=10_000_000_000, bytes_accessed=8_000_000, transcendentals=0
        ),
    )(core.reshape(1), *arrays)


def on_device(
    latent_q,
    latent_kv,
    grad_q_heads,
    grad_kv_heads,
    row_peak,
    momentum_q,
    momentum_kv,
    weight_q,
    weight_kv,
):
    core = lax.axis_index("seq")
    device = core * CHIPS + lax.axis_index("fsdp")
    width_q, rank_q = momentum_q.shape[2], latent_q.shape[1]
    width_kv, rank_kv = momentum_kv.shape[2], latent_kv.shape[1]
    unit = rank_q // LENT
    order = lax.dynamic_index_in_dim(jnp.asarray(block_orders()), device, keepdims=False)
    held = [latent_q[:, :unit], latent_q[:, unit:], latent_kv]
    grad_q = grad_q_heads.T
    send = arrange(1, order, grad_q)
    for phase in range(2):
        for step in range(2):
            if phase + step == 1 and step == 1:
                held = after(held, send[0])
            got = [exchange(held[p], p, phase, step) for p in range(PARTS)]
            got = lax.optimization_barrier(got)
            held = [jnp.concatenate([held[p], got[p]], axis=0) for p in range(PARTS)]
    partner = [exchange(send[p], p, 2, 0) for p in range(LENT)]
    third = [exchange(held[p], p, 2, 1) for p in range(PARTS)]
    second = exchange(held[2], 2, 2, 0)
    fourth = exchange(second, 2, 2, 1)
    order, row_peak, mom_q, mom_kv = after(
        (order, row_peak, momentum_q[0].T, momentum_kv[0]), held[0]
    )
    peaks = (row_peak, swap(row_peak))
    moms_q, moms_kv = (mom_q, swap(mom_q)), (mom_kv, swap(mom_kv))
    keep = arrange(0, order, grad_q)
    grad_kv = line_up(order, grad_kv_heads)
    lent = multiply(0, held[:LENT], partner)
    own = multiply(0, held[:LENT], keep)
    own_kv = multiply(0, held[2:], [grad_kv])
    own_kv = multiply(1, [second], [grad_kv], own_kv)
    own_kv = multiply(2, third[2:], [grad_kv], own_kv)
    lent = multiply(1, third[:LENT], partner, lent)
    got = [exchange(lent[p], p, 2, 0) for p in range(LENT)]
    own = multiply(1, third[:LENT], keep, own)
    (own_kv,) = multiply(3, [fourth], [grad_kv], own_kv)
    new_mom_kv, upd_kv, new_weight_kv = finish(
        finish_kv_kernel,
        (width_kv, rank_kv),
        core,
        own_kv,
        swap(own_kv),
        *peaks,
        *moms_kv,
        weight_kv[0],
    )
    got = after(got, new_mom_kv)
    sums = (*own, *[swap(o) for o in own], *got, *[swap(g) for g in got])
    new_mom_q, upd_q, new_weight_q = finish(
        finish_q_kernel, (width_q, rank_q), core, *sums, *peaks, *moms_q, weight_q[0].T
    )
    return (
        new_mom_q.T[None],
        new_mom_kv[None],
        upd_q.T[None],
        upd_kv[None],
        new_weight_q.T[None],
        new_weight_kv[None],
    )


def solution(mesh):
    rows = P("fsdp", "seq", None)
    placed = (
        P(("seq", "fsdp"), None),
        P(("seq", "fsdp"), None),
        P("seq", "fsdp"),
        P("seq", "fsdp"),
        P("fsdp", "seq"),
        rows,
        rows,
        rows,
        rows,
    )
    return jax.shard_map(
        on_device, mesh=mesh, in_specs=placed, out_specs=(rows,) * 6, check_vma=False
    )
```

```python
import functools
import math

import jax
import jax.numpy as jnp
import numpy as np
from jax import lax
from jax.experimental import pallas as pl
from jax.experimental.pallas import tpu as pltpu
from jax.sharding import PartitionSpec as P

QN = 128
KN = 128
NS_STEPS = 5

coef_a = 3.4445
coef_b = -4.775
coef_c = 2.0315
momentum_rate = 0.95
learn_rate = 0.1
clip_target = 100.0
norm_eps = 1e-07

F32 = jnp.float32
BF16 = jnp.bfloat16

CHIPS = 64
RING = 4
PARTS = 3
LENT = 2
STRIDES = {"z": 16, "y": 4, "x": 1}
AXES = (("xyz", "yzx", "zxy"), ("yzx", "zxy", "xyz"))
HOPS = ((1, 3), (3, 1))
SMEM = pl.BlockSpec(memory_space=pltpu.SMEM)
VMEM = pl.BlockSpec(memory_space=pltpu.VMEM)
MIB = 1024 * 1024


def dot(left, right, left_dim=1, right_dim=0):
    return lax.dot_general(
        left, right, (((left_dim,), (right_dim,)), ((), ())), preferred_element_type=F32
    )


def halves(value):
    high = value.astype(BF16)
    return high, (value - high.astype(F32)).astype(BF16)


def product(left, right):
    (lh, ll), (rh, rl) = left, right
    return dot(lh, rh) + (dot(lh, rl) + dot(ll, rh))


def gram_of(parts):
    high, low = parts
    cross = dot(high, low, 1, 1)
    return dot(high, high, 1, 1) + (cross + cross.T)


def sweep(iterate):
    parts = halves(iterate)
    gram = gram_of(parts)
    gram_parts = halves(gram)
    poly = coef_b * gram + coef_c * product(gram_parts, gram_parts)
    return coef_a * iterate + product(halves(poly), parts)


def normalized(matrix):
    norm = jnp.sqrt(jnp.sum(matrix * matrix, keepdims=True))
    return matrix / (norm + norm_eps)


def swap(value):
    return lax.ppermute(value, "seq", [(0, 1), (1, 0)])


def after(values, earlier):
    return lax.optimization_barrier((values, earlier))[0]


def exchange(value, part, phase, step):
    pairs = []
    for core in range(2):
        stride = STRIDES[AXES[core][part][phase]]
        for chip in range(CHIPS):
            at = chip // stride % RING
            other = chip + ((at ^ HOPS[core][step]) - at) * stride
            pairs.append((core * CHIPS + chip, core * CHIPS + other))
    return lax.ppermute(value, ("seq", "fsdp"), pairs)


def block_orders():
    table = np.zeros((2 * CHIPS, PARTS * CHIPS), np.int32)
    for core in range(2):
        first, second = HOPS[core]
        order = (0, first, second, first ^ second)
        for chip in range(CHIPS):
            for part in range(PARTS):
                for slot in range(CHIPS):
                    chosen = chip
                    for phase in range(3):
                        stride = STRIDES[AXES[core][part][phase]]
                        at = chip // stride % RING
                        turn = order[slot // RING**phase % RING]
                        chosen += ((at ^ turn) - at) * stride
                    table[core * CHIPS + chip, part * CHIPS + slot] = chosen
    return table


def arrange_kernel(first, order_ref, grad_ref, *outs):
    width, tokens = grad_ref.shape
    rows = tokens // CHIPS
    pair = 2 * rows
    left = lax.broadcasted_iota(jnp.int32, (width, pair), 1) < rows

    def joined(one, two):
        turned = []
        for block, half in ((one, 0), (two, 1)):
            tile = grad_ref[:, pl.ds(pl.multiple_of(block // 2 * pair, pair), pair)]
            tile = tile.astype(F32)
            turned.append(jnp.where(block % 2 == half, tile, pltpu.roll(tile, rows, 1)))
        return jnp.where(left, turned[0], turned[1]).astype(BF16)

    for part in range(LENT):
        for slot in (first, first + 2):

            @pl.loop(0, 8)
            def _(at):
                base = part * CHIPS + slot * 16 + at * 2
                lanes = pl.ds(pl.multiple_of((slot // 2 * 8 + at) * pair, pair), pair)
                outs[part][:, lanes] = joined(order_ref[base], order_ref[base + 1])


def arrange(first, order, grad):
    return pl.pallas_call(
        functools.partial(arrange_kernel, first),
        out_shape=(jax.ShapeDtypeStruct((grad.shape[0], grad.shape[1] // 2), BF16),) * LENT,
        in_specs=[SMEM, VMEM],
        out_specs=(VMEM,) * LENT,
        compiler_params=pltpu.CompilerParams(vmem_limit_bytes=12 * MIB),
        cost_estimate=pl.CostEstimate(
            flops=0, bytes_accessed=10_000_000, transcendentals=0
        ),
    )(order, grad)


def line_up_kernel(order_ref, grad_ref, out_ref):
    rows = grad_ref.shape[0] // CHIPS

    @pl.loop(0, CHIPS // RING)
    def _(chunk):
        base = (PARTS - 1) * CHIPS + chunk * RING
        at = [order_ref[base + k] for k in range(RING)]
        spans = [pl.ds(pl.multiple_of(block * rows, rows), rows) for block in at]
        whole = jnp.concatenate([grad_ref[span, :] for span in spans], axis=0)
        lanes = pl.ds(pl.multiple_of(chunk * (RING * rows), RING * rows), RING * rows)
        out_ref[:, lanes] = whole.T


def line_up(order, grad):
    return pl.pallas_call(
        line_up_kernel,
        out_shape=jax.ShapeDtypeStruct(grad.shape[::-1], BF16),
        in_specs=[SMEM, VMEM],
        out_specs=VMEM,
        compiler_params=pltpu.CompilerParams(vmem_limit_bytes=12 * MIB),
        cost_estimate=pl.CostEstimate(
            flops=0, bytes_accessed=10_000_000, transcendentals=0
        ),
    )(order, grad)


def multiply_kernel(slot, count, *refs):
    pieces, grads = refs[:count], refs[count : 2 * count]
    sums, outs = refs[2 * count : -count], refs[-count:]
    for i in range(count):
        span = pieces[i].shape[0]
        term = dot(grads[i][:, slot * span : (slot + 1) * span], pieces[i][...])
        outs[i][...] = term + sums[i][...] if sums else term


def multiply(slot, pieces, grads, sums=()):
    operands = [*pieces, *grads, *sums]
    count = len(pieces)
    return pl.pallas_call(
        functools.partial(multiply_kernel, slot, count),
        out_shape=tuple(
            jax.ShapeDtypeStruct((grad.shape[0], piece.shape[1]), F32)
            for grad, piece in zip(grads, pieces)
        ),
        in_specs=[VMEM] * len(operands),
        out_specs=(VMEM,) * count,
        compiler_params=pltpu.CompilerParams(vmem_limit_bytes=16 * MIB),
        cost_estimate=pl.CostEstimate(
            flops=2_000_000_000, bytes_accessed=8_000_000, transcendentals=0
        ),
    )(*operands)


def clip_factor(peak_ref, peak_other_ref):
    peak = jnp.maximum(
        jnp.max(peak_ref[...], keepdims=True), jnp.max(peak_other_ref[...], keepdims=True)
    )
    return jnp.minimum(1.0, clip_target / peak)


def shares(core_ref, full_ref):
    core, wide = core_ref[0], full_ref.shape[1] // 2
    return tuple(pl.ds(pl.multiple_of(at * wide, 128), wide) for at in (core, 1 - core))


def finish_kernel(core_ref, *refs):
    packs = [refs[i * LENT : (i + 1) * LENT] for i in range(4)]
    rest = refs[4 * LENT :]
    one_kv_ref, two_kv_ref, peak_ref, peak_other_ref = rest[:4]
    mom_q_ref, mom_q_other_ref, mom_kv_ref, mom_kv_other_ref = rest[4:8]
    weight_q_ref, weight_kv_ref = rest[8:10]
    out_mom_q_ref, out_upd_q_ref, out_weight_q_ref = rest[10:13]
    out_mom_kv_ref, out_upd_kv_ref, out_weight_kv_ref, full_q_ref, full_kv_ref = rest[13:]
    own_q, other_q = shares(core_ref, full_q_ref)
    own_kv, other_kv = shares(core_ref, full_kv_ref)
    full_q_ref[:, own_q] = momentum_rate * mom_q_ref[...]
    full_q_ref[:, other_q] = momentum_rate * mom_q_other_ref[...]
    at = 0
    for one, one_swapped, two, two_swapped in zip(*packs):
        wide = one.shape[1]
        full_q_ref[:, at : at + wide] += (one[...] + one_swapped[...]) + (
            two[...] + two_swapped[...]
        )
        at += wide
    full_kv_ref[:, own_kv] = momentum_rate * mom_kv_ref[...].T
    full_kv_ref[:, other_kv] = momentum_rate * mom_kv_other_ref[...].T
    full_kv_ref[...] += one_kv_ref[...] + two_kv_ref[...]
    out_mom_q_ref[...] = full_q_ref[:, own_q]
    out_mom_kv_ref[...] = full_kv_ref[:, own_kv].T
    x_q = normalized(full_q_ref[...])
    x_kv = normalized(full_kv_ref[...])
    for _ in range(NS_STEPS):
        x_q = sweep(x_q)
        x_kv = sweep(x_kv)
    full_q_ref[...] = x_q
    full_kv_ref[...] = x_kv
    factor = clip_factor(peak_ref, peak_other_ref)
    root = jnp.sqrt(factor)
    update_q = (0.2 * math.sqrt(full_q_ref.shape[1])) * full_q_ref[:, own_q]
    out_upd_q_ref[...] = update_q
    rows = lax.broadcasted_iota(jnp.int32, update_q.shape, 0)
    scale_q = jnp.where(rows < QN, root, factor)
    out_weight_q_ref[...] = (weight_q_ref[...] - learn_rate * update_q) * scale_q
    update_kv = ((0.2 * math.sqrt(full_kv_ref.shape[1])) * full_kv_ref[:, own_kv]).T
    out_upd_kv_ref[...] = update_kv
    columns = lax.broadcasted_iota(jnp.int32, update_kv.shape, 1)
    scale_kv = jnp.where(columns < KN, root, 1.0)
    out_weight_kv_ref[...] = (weight_kv_ref[...] - learn_rate * update_kv) * scale_kv


def finish(core, *arrays):
    weight_q, weight_kv = arrays[-2:]
    shape_q = jax.ShapeDtypeStruct(weight_q.shape, F32)
    shape_kv = jax.ShapeDtypeStruct(weight_kv.shape, F32)
    return pl.pallas_call(
        finish_kernel,
        out_shape=(shape_q,) * 3 + (shape_kv,) * 3,
        in_specs=[SMEM] + [VMEM] * len(arrays),
        out_specs=(VMEM,) * 6,
        scratch_shapes=[
            pltpu.VMEM((weight_q.shape[0], 2 * weight_q.shape[1]), F32),
            pltpu.VMEM((weight_kv.shape[1], 2 * weight_kv.shape[0]), F32),
        ],
        compiler_params=pltpu.CompilerParams(vmem_limit_bytes=20 * MIB),
        cost_estimate=pl.CostEstimate(
            flops=20_000_000_000, bytes_accessed=12_000_000, transcendentals=0
        ),
    )(core.reshape(1), *arrays)


def on_device(
    latent_q,
    latent_kv,
    grad_q_heads,
    grad_kv_heads,
    row_peak,
    momentum_q,
    momentum_kv,
    weight_q,
    weight_kv,
):
    core = lax.axis_index("seq")
    device = core * CHIPS + lax.axis_index("fsdp")
    unit = latent_q.shape[1] // LENT
    order = lax.dynamic_index_in_dim(jnp.asarray(block_orders()), device, keepdims=False)
    held = [latent_q[:, :unit], latent_q[:, unit:], latent_kv]
    grad_q = grad_q_heads.T
    send = arrange(1, order, grad_q)
    for phase in range(2):
        for step in range(2):
            if phase + step == 1 and step == 1:
                held = after(held, send[0])
            got = [exchange(held[p], p, phase, step) for p in range(PARTS)]
            got = lax.optimization_barrier(got)
            held = [jnp.concatenate([held[p], got[p]], axis=0) for p in range(PARTS)]
    partner = [exchange(send[p], p, 2, 0) for p in range(LENT)]
    third = [exchange(held[p], p, 2, 1) for p in range(LENT)]
    third.append(exchange(after(held[2], partner[0]), 2, 2, 1))
    second = exchange(held[2], 2, 2, 0)
    order, row_peak, mom_q, mom_kv = after(
        (order, row_peak, momentum_q[0].T, momentum_kv[0]), held[0]
    )
    peaks = (row_peak, swap(row_peak))
    moms_q, moms_kv = (mom_q, swap(mom_q)), (mom_kv, swap(mom_kv))
    keep = arrange(0, order, grad_q)
    grad_kv = line_up(order, grad_kv_heads)
    fourth = [
        exchange(after(second, (keep, grad_kv))[: second.shape[0] // 2], 2, 2, 1),
        exchange(after(third[2], partner)[third[2].shape[0] // 2 :], 2, 2, 0),
    ]
    lent = multiply(0, held[:LENT], partner)
    own = multiply(0, held[:LENT], keep)
    own_kv = multiply(0, held[2:], [grad_kv])
    own_kv = multiply(1, [second], [grad_kv], own_kv)
    own_kv = multiply(2, third[2:], [grad_kv], own_kv)
    lent = multiply(1, third[:LENT], partner, lent)
    got = [exchange(lent[p], p, 2, 0) for p in range(LENT)]
    own = multiply(1, third[:LENT], keep, own)
    own_kv = multiply(6, fourth[:1], [grad_kv], own_kv)
    (own_kv,) = multiply(7, fourth[1:], [grad_kv], own_kv)
    sums = (*own, *[swap(o) for o in own], *got, *[swap(g) for g in got])
    outs = finish(
        core,
        *sums,
        own_kv,
        swap(own_kv),
        *peaks,
        *moms_q,
        *moms_kv,
        weight_q[0].T,
        weight_kv[0],
    )
    new_mom_q, upd_q, new_weight_q, new_mom_kv, upd_kv, new_weight_kv = outs
    return (
        new_mom_q.T[None],
        new_mom_kv[None],
        upd_q.T[None],
        upd_kv[None],
        new_weight_q.T[None],
        new_weight_kv[None],
    )


def solution(mesh):
    rows = P("fsdp", "seq", None)
    placed = (
        P(("seq", "fsdp"), None),
        P(("seq", "fsdp"), None),
        P("seq", "fsdp"),
        P("seq", "fsdp"),
        P("fsdp", "seq"),
        rows,
        rows,
        rows,
        rows,
    )
    return jax.shard_map(
        on_device, mesh=mesh, in_specs=placed, out_specs=(rows,) * 6, check_vma=False
    )
```
